256 devices in a mesh: img: 32 (over z, x_lo, core), phr: 8 (over x_hi, y).
Axes of the slice: x: 4 (x_hi: 2, x_lo: 2; x = x_hi * 2 + x_lo), y: 4, z: 8, core: 2. Of those that a mesh axis runs over, the one named last changes fastest.
Arguments:
- image_cell_features: bfloat16 [2048, 256, 1152], P(('img', 'phr')), may hold values from -0.29882812 to 0.29882812
- area_rectangle_limits: int32 [24576, 4], P(('img', 'phr')), may hold values from 0 to 16, as said below
- area_shard_index: int32 [24576], replicated, may hold values from 0 to 31, as said below
- caption_described_area: int32 [98304], replicated, may hold values from 0 to 24575, as said below
- caption_embeddings: bfloat16 [98304, 1152], P(('img', 'phr')), may hold values from -6 to 6
- sharpness_multiplier: float32 [1], replicated, may hold values from 20 to 40
- sigmoid_shift_term: float32 [1], replicated, may hold values from -4 to -2
Outputs:
- patch_grad: bfloat16 [2048, 256, 1152], P(('img', 'phr'))
The draws below stay inside these ranges and needn't reach their ends.
Inputs may be any that keep to these rules, and one draw needn't show every extreme that they name: `area_rectangle_limits`: each row is a box of at least one patch: first row < end row, first column < end column. Region k of a device lies in that device's image k // 12. `area_shard_index`: among the 96 regions of one device at most 7 go to any one shard; in every draw every device sends exactly 7 to some shard. `caption_described_area`: phrase p names a region assigned to shard p // 3072 whenever that shard has any region.
All inputs are finite; a program needn't handle non-finite values.
Results may differ from the reference program's by a relative error of at most 0.01.
Values may be sent and summed in bfloat16 or wider, within the bound.
A program may use at most 64 MiB of HBM per device.

```python
import jax
import jax.numpy as jnp
from jax import lax

D = 1152
GRID = 16
REG_IMG = 12
REG_DEV = 96
PH_DEV = 384
CAP = 7
PATCHES = 256
IMAGES = 2048
REGIONS = 24576
PHRASES = 98304
N_IMG = 32
N_PHR = 8
DEVICES = 256


def shared_assignment(key):
    devices_all = N_IMG * N_PHR
    slot_total = N_IMG * CAP
    subkeys = jax.random.split(jax.random.fold_in(key, 11), devices_all)
    orders = jax.vmap(lambda subkey: jax.random.permutation(subkey, slot_total))(subkeys)
    full_shard = jax.random.randint(jax.random.fold_in(key, 12), (devices_all, 1), 0, N_IMG)
    slot_shard = jnp.arange(slot_total, dtype=jnp.int32) // CAP
    scores = orders.astype(jnp.int32) + jnp.where(slot_shard[None, :] == full_shard, 0, slot_total)
    picked = jnp.argsort(scores, axis=1)[:, :REG_DEV].astype(jnp.int32)
    mix_keys = jax.random.split(jax.random.fold_in(key, 13), devices_all)
    picked = jax.vmap(lambda subkey, row_vals: jax.random.permutation(subkey, row_vals))(mix_keys, picked)
    return (picked // CAP).reshape(-1).astype(jnp.int32)


def draw_area_shard_index(key, part):
    shard_ids = shared_assignment(key)
    return shard_ids


def draw_caption_described_area(key, part):
    shard_ids = shared_assignment(key)
    key = jax.random.fold_in(key, 2)
    row_len = N_PHR * PH_DEV
    subkeys = jax.random.split(key, N_IMG)
    shuffled = jax.vmap(lambda subkey: jax.random.permutation(subkey, REGIONS))(subkeys).astype(jnp.int32)
    row_ids = jnp.arange(N_IMG, dtype=jnp.int32)
    member = shard_ids[None, :] == row_ids[:, None]
    scores = shuffled + jnp.where(member, 0, REGIONS)
    order = jnp.argsort(scores, axis=1).astype(jnp.int32)
    counts = jnp.sum(member.astype(jnp.int32), axis=1)
    wanted = jnp.arange(row_len, dtype=jnp.int32)[None, :] % jnp.maximum(counts, 1)[:, None]
    return jnp.take_along_axis(order, wanted, axis=1).reshape(-1).astype(jnp.int32)


def draw_area_rectangle_limits(key, part):
    key = jax.random.fold_in(key, 3)
    row_key, col_key = jax.random.split(key)
    row_pair = jax.random.randint(row_key, (REGIONS, 2), 0, GRID)
    col_pair = jax.random.randint(col_key, (REGIONS, 2), 0, GRID)
    spans = jnp.stack([jnp.min(row_pair, axis=1), jnp.max(row_pair, axis=1) + 1, jnp.min(col_pair, axis=1), jnp.max(col_pair, axis=1) + 1], axis=1)
    return spans.astype(jnp.int32)


def levels(key, dims, shards, low, top_value):
    loudness, own = 1.0, jax.random.fold_in(key, 6)
    for dim, blocks in shards:
        steps = jnp.exp(jax.random.uniform(jax.random.fold_in(own, dim), (blocks,), jnp.float32, low / len(shards), top_value / len(shards)))
        loudness = loudness * jnp.repeat(steps, dims[dim] // blocks).reshape([-1 if axis == dim else 1 for axis in range(len(dims))])
    return loudness


def gaussian(rng, shape, deviation, reach, shards=(), kind=jnp.bfloat16):
    level = levels(rng, shape, shards, -0.22, 0.18) if shards else 1.0
    result = jax.random.normal(rng, shape, jnp.float32) * deviation * level
    return jnp.minimum(jnp.maximum(result, -reach), reach).astype(kind)


def setup_inputs(seed: int = 0) -> dict:
    key_of = jax.random.split(jax.random.key(seed), 8)
    image_cell_features = gaussian(key_of[0], (IMAGES, PATCHES, D), 0.05, 0.29882812, ((0, 256),))
    area_rectangle_limits = draw_area_rectangle_limits(jax.random.fold_in(key_of[7], 71), 0)
    area_shard_index = draw_area_shard_index(jax.random.fold_in(key_of[7], 71), 0)
    caption_described_area = draw_caption_described_area(jax.random.fold_in(key_of[7], 71), 0)
    caption_embeddings = gaussian(key_of[4], (PHRASES, D), 1.0, 6.0, ((0, 256),))
    sharpness_multiplier = jnp.clip(jax.random.uniform(key_of[5], (1,), jnp.float32, 20.0, 40.0), 20.0, 40.0)
    sigmoid_shift_term = jnp.clip(jax.random.uniform(key_of[6], (1,), jnp.float32, -4.0, -2.0), -4.0, -2.0)
    return dict(image_cell_features=image_cell_features, area_rectangle_limits=area_rectangle_limits, area_shard_index=area_shard_index, caption_described_area=caption_described_area, caption_embeddings=caption_embeddings, sharpness_multiplier=sharpness_multiplier, sigmoid_shift_term=sigmoid_shift_term)


epsilon = 1e-06

def reference(image_cell_features, area_rectangle_limits, area_shard_index, caption_described_area, caption_embeddings, sharpness_multiplier, sigmoid_shift_term):
    spot_ids = jnp.arange(PATCHES, dtype=jnp.int32)
    patch_row = spot_ids // GRID
    patch_col = spot_ids % GRID
    corners = area_rectangle_limits.reshape(IMAGES, REG_IMG, 4)
    inside = ((patch_row >= corners[:, :, 0:1]) & (patch_row < corners[:, :, 1:2]) & (patch_col >= corners[:, :, 2:3]) & (patch_col < corners[:, :, 3:4])).astype(jnp.bfloat16)

    def pool_one(item_pair):
        return jnp.dot(item_pair[0], item_pair[1], preferred_element_type=jnp.float32)
    pooled = lax.map(pool_one, (inside, image_cell_features)).reshape(REGIONS, D).astype(jnp.bfloat16)
    pooled_f = pooled.astype(jnp.float32)
    inverse = lax.rsqrt(lax.optimization_barrier(jnp.sum(pooled_f * pooled_f, axis=1, keepdims=True)) + epsilon)
    region_unit = (pooled_f * inverse).astype(jnp.bfloat16)
    phrase_f = caption_embeddings.astype(jnp.float32)
    phrase_unit = (phrase_f * lax.rsqrt(lax.optimization_barrier(jnp.sum(phrase_f * phrase_f, axis=1, keepdims=True)) + epsilon)).astype(jnp.bfloat16)
    blocks = area_shard_index.reshape(DEVICES, REG_DEV)
    local_ids = jnp.arange(REG_DEV, dtype=jnp.int32)
    earlier = local_ids[None, :] < local_ids[:, None]
    ranks = lax.optimization_barrier(jnp.sum(((blocks[:, :, None] == blocks[:, None, :]) & earlier[None]).astype(jnp.int32), axis=2)).reshape(REGIONS)
    region_ids = jnp.arange(REGIONS, dtype=jnp.int32)
    source = region_ids // REG_DEV
    slot_global = (((area_shard_index * N_PHR + source % N_PHR) * N_IMG + source // N_PHR) * CAP + ranks).astype(jnp.int32)
    row_slots = N_PHR * N_IMG * CAP
    occupant = jnp.full((N_IMG * row_slots,), -1, jnp.int32).at[slot_global].set(region_ids)
    row_len = N_PHR * PH_DEV

    def shard_terms(shard_id):
        present = lax.dynamic_slice_in_dim(occupant, (shard_id * row_slots).astype(jnp.int32), row_slots)
        usable = (present >= 0).astype(jnp.float32)
        direction_embeddings = jnp.where(present[:, None] >= 0, region_unit[jnp.maximum(present, 0)], jnp.zeros((), jnp.bfloat16)).astype(jnp.bfloat16)
        start_row = (shard_id * row_len).astype(jnp.int32)
        tile_direction_rows = lax.dynamic_slice_in_dim(phrase_unit, start_row, row_len)
        named_ids = lax.dynamic_slice_in_dim(caption_described_area, start_row, row_len)
        similarity_grid_scores = sharpness_multiplier[0] * lax.dot_general(direction_embeddings, tile_direction_rows, (((1,), (1,)), ((), ())), preferred_element_type=jnp.float32) + sigmoid_shift_term[0]
        positive = named_ids[None, :] == present[:, None]
        averaging_coefficient = ((jax.nn.sigmoid(similarity_grid_scores) - positive.astype(jnp.float32)) * usable[:, None]).astype(jnp.bfloat16)
        return sharpness_multiplier[0] * jnp.dot(averaging_coefficient, tile_direction_rows, preferred_element_type=jnp.float32)
    pulls = lax.map(shard_terms, jnp.arange(N_IMG, dtype=jnp.int32))
    pull = pulls.reshape(N_IMG * row_slots, D)[slot_global]
    radial = lax.optimization_barrier(jnp.sum(pooled_f * pull, axis=1, keepdims=True))
    region_pull = inverse * pull - inverse ** 3 * radial * pooled_f

    def spread_one(item_pair):
        return jnp.dot(item_pair[0].astype(jnp.float32).T, item_pair[1], precision=lax.Precision.HIGHEST, preferred_element_type=jnp.float32)
    patch_grad = lax.map(spread_one, (inside, region_pull.reshape(IMAGES, REG_IMG, D))).astype(jnp.bfloat16)
    return patch_grad
```

```python
import jax
import jax.numpy as jnp
from jax import lax
from jax.experimental import pallas as pl
from jax.experimental.pallas import tpu as pltpu
from jax.sharding import PartitionSpec as P

MESH = pl.DeviceIdType.MESH
GRID = 16
NZ, NX, NY = 8, 4, 4
SLOT = 8
EPS = 1e-06
BF16, F32, I32 = jnp.bfloat16, jnp.float32, jnp.int32

ORDER = (4, 3, 5, 2, 6, 1, 7, 0)
PLACE = {rel: k for k, rel in enumerate(ORDER)}


def place():
    img, phr = lax.axis_index("img"), lax.axis_index("phr")
    return img // 4, (phr // 4) * 2 + (img // 2) % 2, phr % 4, img % 2


def device_at(z, x, y, c):
    z, x, y, c = lax.rem(z, NZ), lax.rem(x, NX), lax.rem(y, NY), lax.rem(c, 2)
    return ((z * 2 + lax.rem(x, 2)) * 2 + c, (x // 2) * 4 + y)


def iota(shape, dim):
    return lax.broadcasted_iota(I32, shape, dim)


def dot(a, b):
    return jnp.dot(a, b, preferred_element_type=F32)


def exchange_kernel(
    sharp_ref,
    shift_ref,
    limits_ref,
    shard_ref,
    named_hbm,
    phrase_hbm,
    feature_hbm,
    back_ref,
    spread_ref,
    feature,
    raw,
    named,
    phrases,
    pool,
    z_out,
    z_in,
    x_out,
    x_in,
    unit,
    ids,
    inverse,
    total,
    p_out,
    p_in,
    s_out,
    in_sem,
    feature_sem,
    y_send,
    y_recv,
    zf_send,
    zf_recv,
    xf_send,
    xf_recv,
    xr_send,
    xr_recv,
    zr_send,
    zr_recv,
):
    z, x, y, c = place()
    me_img, me_phr = lax.axis_index("img"), lax.axis_index("phr")
    shard = me_img
    reg_dev = limits_ref.shape[0]
    n_dev = shard_ref.shape[0]
    ph_dev = raw.shape[0]
    half = ph_dev // 2
    reg_img = 12
    patches = GRID * GRID
    n_feature = feature_sem.shape[0]
    chunk = feature.shape[0] // n_feature

    def remote(src, dst, send, recv, dz=0, dx=0, dy=0, dc=0):
        return pltpu.make_async_remote_copy(
            src_ref=src,
            dst_ref=dst,
            send_sem=send,
            recv_sem=recv,
            device_id=device_at(z + dz % NZ, x + dx % NX, y + dy % NY, c + dc),
            device_id_type=MESH,
        )

    phrase_copy = pltpu.make_async_copy(phrase_hbm, raw, in_sem.at[0])
    phrase_copy.start()
    feature_copies = []
    for i in range(n_feature):
        rows = pl.ds(i * chunk, chunk)
        copy = pltpu.make_async_copy(feature_hbm.at[rows], feature.at[rows], feature_sem.at[i])
        copy.start()
        feature_copies.append(copy)
    named_copy = pltpu.make_async_copy(named_hbm.at[pl.ds(shard * 24, 24)], named, in_sem.at[1])
    named_copy.start()

    barrier = pltpu.get_barrier_semaphore()
    partners = [(dz, 0, 0, dc) for dz in range(NZ) for dc in range(2) if (dz, dc) != (0, 0)]
    partners += [(0, dx, 0, 0) for dx in range(1, NX)] + [(0, 0, 1, 0), (0, 0, 3, 0)]
    for dz, dx, dy, dc in partners:
        pl.semaphore_signal(
            barrier, inc=1, device_id=device_at(z + dz, x + dx, y + dy, c + dc), device_id_type=MESH
        )

    phrase_copy.wait()
    for i in range(0, ph_dev, 64):
        rows = pl.ds(i, 64)
        own = raw[rows].astype(F32)
        scale = lax.rsqrt(jnp.sum(own * own, axis=1, keepdims=True) + EPS)
        phrases[rows] = (own * scale).astype(BF16)
    pl.semaphore_wait(barrier, len(partners))

    def part(block, which):
        return phrases.at[pl.ds(block * ph_dev + which * half, half)]

    def ring(index, src, dst, dy):
        return remote(src, dst, y_send.at[index], y_recv.at[index], dy=dy)

    ring_copies = [
        ring(0, part(0, 0), part(1, 0), 1),
        ring(1, part(0, 1), part(2, 1), -1),
        ring(2, part(0, 1), part(1, 1), 1),
        ring(3, part(0, 0), part(2, 0), -1),
        ring(4, part(1, 0), part(3, 0), 1),
        ring(5, part(2, 1), part(3, 1), -1),
    ]
    for copy in ring_copies[:4]:
        copy.start()

    own = shard_ref[pl.ds(me_img * 8 + me_phr, 1), :]
    member = (iota((32, reg_dev), 0) == own).astype(F32)
    earlier = (iota((reg_dev, reg_dev), 0) < iota((reg_dev, reg_dev), 1)).astype(BF16)
    rank = jnp.sum(member * dot(member.astype(BF16), earlier), axis=0, keepdims=True).astype(I32)
    parity = lax.rem(x, 2)
    to_z = ((own >> 2) - z + NZ) & (NZ - 1)
    to_c = jnp.where((own & 1) == c, 0, 1)
    to_x = jnp.where(((own >> 1) & 1) == parity, 0, 1)
    goes = ((to_z * 2 + to_c) * 2 + to_x) * SLOT + rank
    slots = NZ * 4 * SLOT
    dispatch = (iota((slots, reg_dev), 0) == goes).astype(BF16)

    spot = iota((reg_dev, patches), 1)
    spot_row, spot_col = spot >> 4, spot & 15
    inside = (
        (spot_row >= limits_ref[:, 0:1])
        & (spot_row < limits_ref[:, 1:2])
        & (spot_col >= limits_ref[:, 2:3])
        & (spot_col < limits_ref[:, 3:4])
    )
    region = iota((reg_dev, patches), 0)
    images = chunk // patches
    for i in range(n_feature):
        feature_copies[i].wait()
        mask = jnp.concatenate(
            [
                (
                    inside
                    & (region >= (i * images + m) * reg_img)
                    & (region < (i * images + m + 1) * reg_img)
                ).astype(F32)
                for m in range(images)
            ],
            axis=1,
        ).astype(BF16)
        term = dot(mask, feature[pl.ds(i * chunk, chunk)])
        pool[...] = term if i == 0 else pool[...] + term
    z_out[...] = dot(dispatch, pool[...].astype(BF16)).astype(BF16)

    def block(ref, index):
        return ref.at[pl.ds(index * 2 * SLOT, 2 * SLOT)]

    z_copies = {}
    for dz in ORDER:
        for dc in range(2):
            if (dz, dc) == (0, 0):
                continue
            there = (NZ - dz) % NZ
            copy = remote(
                block(z_out, dz * 2 + dc),
                block(z_in, there * 2 + dc),
                zf_send.at[dz, dc],
                zf_recv.at[there, dc],
                dz=dz,
                dc=dc,
            )
            copy.start()
            z_copies[dz, dc] = copy

    live = 4 * NZ * 2 * SLOT
    member_all = (shard_ref[...] == shard).astype(BF16)
    rank_all = dot(member_all, earlier).astype(BF16)
    slot = iota((live, n_dev), 0)
    k, xr, dc_, r_ = slot >> 6, (slot >> 4) & 3, (slot >> 3) & 1, slot & 7
    rel = jnp.zeros_like(k)
    for rel_z, at in PLACE.items():
        rel = jnp.where(k == at, rel_z, rel)
    from_z = (z + rel) & (NZ - 1)
    from_x = (x + xr) & (NX - 1)
    from_c = (c + dc_) & 1
    device = ((from_z * 2 + (from_x & 1)) * 2 + from_c) * 8 + (from_x >> 1) * 4 + y
    pick = (iota((live, n_dev), 1) == device).astype(BF16)
    member_slot = dot(pick, member_all)
    rank_slot = dot(pick, rank_all)
    wanted = r_[:, :reg_dev].astype(F32)
    local = (iota((live, reg_dev), 1) + 1).astype(F32)
    held = jnp.sum(
        jnp.where(rank_slot == wanted, member_slot * local, 0.0), axis=1, keepdims=True
    ).astype(I32)
    ids[...] = jnp.where(held > 0, device[:, :128] * reg_dev + held - 1, -1)

    same = iota((reg_dev, reg_dev), 0) == iota((reg_dev, reg_dev), 1)
    goes_column = jnp.sum(
        jnp.where(same, goes.astype(F32), 0.0), axis=1, keepdims=True
    ).astype(I32)
    collect = (iota((reg_dev, slots), 1) == goes_column).astype(BF16)
    spot = iota((patches, reg_dev), 0)
    spot_row, spot_col = spot >> 4, spot & 15
    limit = [
        jnp.sum(
            jnp.where(same, limits_ref[:, j : j + 1].astype(F32), 0.0), axis=0, keepdims=True
        ).astype(I32)
        for j in range(4)
    ]
    inside = (
        (spot_row >= limit[0])
        & (spot_row < limit[1])
        & (spot_col >= limit[2])
        & (spot_col < limit[3])
    )
    region = iota((patches, reg_dev), 1)
    for m in range(reg_dev // reg_img):
        mask = (inside & (region >= m * reg_img) & (region < (m + 1) * reg_img)).astype(BF16)
        spread_ref[pl.ds(m * patches, patches)] = dot(mask, collect).astype(BF16)

    ring_copies[0].wait_recv()
    ring_copies[4].start()
    ring_copies[1].wait_recv()
    ring_copies[5].start()

    x_copies = {}
    for at, rel_z in enumerate(ORDER):
        sides = []
        for dc in range(2):
            if (rel_z, dc) == (0, 0):
                got = block(z_out, 0)
            else:
                got = block(z_in, rel_z * 2 + dc)
                z_copies[(NZ - rel_z) % NZ, dc].wait_recv()
            sides.append(got[...].astype(F32))
        near, far = [
            jnp.concatenate(
                [side[p * SLOT : (p + 1) * SLOT] for side in sides], axis=0
            ).astype(BF16)
            for p in range(2)
        ]
        block(x_in, at * 4)[...] = near
        block(x_out, at * 2)[...] = near
        block(x_out, at * 2 + 1)[...] = far
        for dx in (2, 1, 3):
            there = NX - dx
            copy = remote(
                block(x_out, at * 2 + dx % 2),
                block(x_in, at * 4 + there),
                xf_send.at[at, dx - 1],
                xf_recv.at[at, there - 1],
                dx=dx,
            )
            copy.start()
            x_copies[at, dx] = copy

    named_copy.wait()
    sharp, shift = sharp_ref[0], shift_ref[0]
    for at in range(NZ):
        for dx in (2, 1, 3):
            x_copies[at, dx].wait_recv()
        rows = pl.ds(at * 64, 64)
        arrived = x_in[rows].astype(F32)
        inv = lax.rsqrt(jnp.sum(arrived * arrived, axis=1, keepdims=True) + EPS)
        inverse[rows] = jnp.broadcast_to(inv, (64, 128))
        unit[rows] = (arrived * inv).astype(BF16)

    def pairs(rows, count, which, dy):
        them = phrases[pl.ds(which * ph_dev, ph_dev)]
        scores = lax.dot_general(
            unit[rows], them, (((1,), (1,)), ((), ())), preferred_element_type=F32
        )
        first = (me_phr // 4) * 12 + lax.rem(y + dy, NY) * 3
        mine = ids[rows]
        weights = []
        for j in range(ph_dev // 128):
            logits = sharp * scores[:, j * 128 : (j + 1) * 128] + shift
            positive = (mine == named[pl.ds(first + j, 1), :]).astype(F32)
            weights.append((jax.nn.sigmoid(logits) - positive).astype(BF16))
        return dot(jnp.concatenate(weights, axis=1), them)

    everything = pl.ds(0, live)
    total[...] = pairs(everything, live, 0, 0)
    ring_copies[2].wait_recv()
    total[...] += pairs(everything, live, 1, 3)
    ring_copies[3].wait_recv()
    total[...] += pairs(everything, live, 2, 1)
    ring_copies[4].wait_recv()
    ring_copies[5].wait_recv()
    r_copies = {}
    for part_rows in range(2):
        rows = pl.ds(part_rows * (live // 2), live // 2)
        total[rows] += pairs(rows, live // 2, 3, 2)
        for at in range(part_rows * 4, part_rows * 4 + 4):
            rows = pl.ds(at * 64, 64)
            pull = sharp * total[rows]
            arrived = x_in[rows].astype(F32)
            inv = inverse[rows][:, 0:1]
            radial = jnp.sum(arrived * pull, axis=1, keepdims=True)
            p_out[rows] = (inv * pull - (inv * inv * inv * radial) * arrived).astype(BF16)
            for dx in (2, 1, 3):
                there = NX - dx
                copy = remote(
                    block(p_out, at * 4 + dx),
                    block(p_in, at * 4 + there),
                    xr_send.at[at, dx - 1],
                    xr_recv.at[at, there - 1],
                    dx=dx,
                )
                copy.start()
                r_copies[at, dx] = copy

    home_copies = {}
    for at, rel_z in enumerate(ORDER):
        for dx in (2, 1, 3):
            r_copies[at, dx].wait_recv()
        near = block(p_out, at * 4)[...].astype(F32) + block(p_in, at * 4 + 2)[...].astype(F32)
        far = block(p_in, at * 4 + 1)[...].astype(F32) + block(p_in, at * 4 + 3)[...].astype(F32)
        there = (NZ - rel_z) % NZ
        for dc in range(2):
            rows = slice(dc * SLOT, (dc + 1) * SLOT)
            both = jnp.concatenate([near[rows], far[rows]], axis=0).astype(BF16)
            if (rel_z, dc) == (0, 0):
                block(back_ref, 0)[...] = both
                continue
            block(s_out, rel_z * 2 + dc)[...] = both
            copy = remote(
                block(s_out, rel_z * 2 + dc),
                block(back_ref, there * 2 + dc),
                zr_send.at[rel_z, dc],
                zr_recv.at[there, dc],
                dz=rel_z,
                dc=dc,
            )
            copy.start()
            home_copies[rel_z, dc] = copy

    for copy in home_copies.values():
        copy.wait_recv()
    for copies in (ring_copies, z_copies.values(), x_copies.values(), r_copies.values(), home_copies.values()):
        for copy in copies:
            copy.wait_send()


def spread_kernel(spread_ref, back_ref, out_ref):
    out_ref[0] = dot(spread_ref[...], back_ref[...]).astype(BF16)


def shards(features, limits, shard_index, named, phrases, sharpness, shift):
    images, patches, width = features.shape
    reg_dev, ph_dev = limits.shape[0], phrases.shape[0]
    slots = NZ * 4 * SLOT
    live = slots * 2
    vmem = pl.BlockSpec(memory_space=pltpu.VMEM)
    smem = pl.BlockSpec(memory_space=pltpu.SMEM)
    anywhere = pl.BlockSpec(memory_space=pl.ANY)
    dma = pltpu.SemaphoreType.DMA
    back, spread = pl.pallas_call(
        exchange_kernel,
        out_shape=(
            jax.ShapeDtypeStruct((slots, width), BF16),
            jax.ShapeDtypeStruct((images * patches, slots), BF16),
        ),
        in_specs=[smem, smem, vmem, vmem, anywhere, anywhere, anywhere],
        out_specs=(vmem, vmem),
        scratch_shapes=[
            pltpu.VMEM((images * patches, width), BF16),
            pltpu.VMEM((ph_dev, width), BF16),
            pltpu.VMEM((24, 128), I32),
            pltpu.VMEM((NY * ph_dev, width), BF16),
            pltpu.VMEM((reg_dev, width), F32),
            pltpu.VMEM((slots, width), BF16),
            pltpu.VMEM((slots, width), BF16),
            pltpu.VMEM((slots, width), BF16),
            pltpu.VMEM((live, width), BF16),
            pltpu.VMEM((live, width), BF16),
            pltpu.VMEM((live, 128), I32),
            pltpu.VMEM((live, 128), F32),
            pltpu.VMEM((live, width), F32),
            pltpu.VMEM((live, width), BF16),
            pltpu.VMEM((live, width), BF16),
            pltpu.VMEM((slots, width), BF16),
            dma((2,)),
            dma((4,)),
            dma((6,)),
            dma((6,)),
            dma((NZ, 2)),
            dma((NZ, 2)),
            dma((NZ, 3)),
            dma((NZ, 3)),
            dma((NZ, 3)),
            dma((NZ, 3)),
            dma((NZ, 2)),
            dma((NZ, 2)),
        ],
        compiler_params=pltpu.CompilerParams(
            collective_id=0, has_side_effects=True, vmem_limit_bytes=50 * 2**20
        ),
    )(
        sharpness,
        shift,
        limits,
        shard_index.reshape(-1, reg_dev),
        named.reshape(-1, 128),
        phrases,
        features.reshape(images * patches, width),
    )
    return pl.pallas_call(
        spread_kernel,
        grid=(images,),
        out_shape=jax.ShapeDtypeStruct((images, patches, width), BF16),
        in_specs=[
            pl.BlockSpec((patches, slots), lambda m: (m, 0)),
            pl.BlockSpec((slots, width), lambda m: (0, 0)),
        ],
        out_specs=pl.BlockSpec((1, patches, width), lambda m: (m, 0, 0)),
    )(spread, back)


def solution(mesh):
    return jax.shard_map(
        shards,
        mesh=mesh,
        in_specs=(
            P(("img", "phr"), None, None),
            P(("img", "phr"), None),
            P(),
            P(),
            P(("img", "phr"), None),
            P(),
            P(),
        ),
        out_specs=P(("img", "phr"), None, None),
        check_vma=False,
    )
```

```python
import jax
import jax.numpy as jnp
from jax import lax
from jax.experimental import pallas as pl
from jax.experimental.pallas import tpu as pltpu
from jax.sharding import PartitionSpec as P

MESH = pl.DeviceIdType.MESH
GRID = 16
NZ, NX, NY = 8, 4, 4
SLOT = 8
EPS = 1e-06
BF16, F32, I32 = jnp.bfloat16, jnp.float32, jnp.int32

ORDER = (4, 3, 5, 2, 6, 1, 7, 0)
PLACE = {rel: k for k, rel in enumerate(ORDER)}
NEAR = (0, 1, 7, 2, 6, 3, 5, 4)
ISSUE = NEAR
POOL_EARLY = 2
LATE_OWN = 1
LATE_PASS = 2
LATE_REST = 4
LANES = 128


def place():
    img, phr = lax.axis_index("img"), lax.axis_index("phr")
    return img // 4, (phr // 4) * 2 + (img // 2) % 2, phr % 4, img % 2


def device_at(z, x, y, c):
    z, x, y, c = lax.rem(z, NZ), lax.rem(x, NX), lax.rem(y, NY), lax.rem(c, 2)
    return ((z * 2 + lax.rem(x, 2)) * 2 + c, (x // 2) * 4 + y)


def iota(shape, dim):
    return lax.broadcasted_iota(I32, shape, dim)


def dot(a, b):
    return jnp.dot(a, b, preferred_element_type=F32)


def fold(value):
    groups, keep = value.shape[0] // SLOT, value.shape[1] - LANES
    value = value.reshape(groups, SLOT, keep + LANES)
    tiles = [value[:, t : t + 1, keep:] for t in range(SLOT - 1)]
    tiles.append(jnp.zeros((groups, 1, keep - (SLOT - 1) * LANES), F32))
    spare = iota((groups, SLOT, keep), 1) == SLOT - 1
    folded = jnp.where(spare, jnp.concatenate(tiles, axis=2), value[:, :, :keep])
    return folded.reshape(groups * SLOT, keep)


def folded_columns(folded):
    groups, keep = folded.shape[0] // SLOT, folded.shape[1]
    folded = folded.reshape(groups, SLOT, keep)
    row = iota((groups, SLOT, LANES), 1)
    columns = jnp.zeros((groups, SLOT, LANES), F32)
    for t in range(SLOT - 1):
        tile = folded[:, SLOT - 1 : SLOT, t * LANES : (t + 1) * LANES]
        columns = jnp.where(row == t, tile, columns)
    return columns.reshape(groups * SLOT, LANES)


def exchange_kernel(
    sharp_hbm,
    shift_hbm,
    limits_hbm,
    shard_hbm,
    named_hbm,
    phrase_hbm,
    feature_hbm,
    back_hbm,
    spread_hbm,
    feature,
    raw,
    named,
    sharp_ref,
    shift_ref,
    limits_ref,
    flat_ref,
    shard_ref,
    phrases,
    pool,
    z_out,
    z_in,
    x_out,
    x_in,
    regions,
    unit,
    ids,
    inverse,
    total,
    p_out,
    p_in,
    s_out,
    spread,
    in_sem,
    feature_sem,
    y_send,
    y_recv,
    zf_send,
    zf_recv,
    xf_send,
    xf_recv,
    xr_send,
    xr_recv,
    zr_send,
    zr_recv,
):
    z, x, y, c = place()
    me_img, me_phr = lax.axis_index("img"), lax.axis_index("phr")
    shard = me_img
    reg_dev = limits_ref.shape[1]
    n_dev = shard_ref.shape[0]
    ph_dev = raw.shape[0]
    half = ph_dev // 2
    reg_img = 12
    patches = GRID * GRID
    n_feature = feature_sem.shape[0]
    chunk = feature.shape[0] // n_feature

    def remote(src, dst, send, recv, dz=0, dx=0, dy=0, dc=0):
        return pltpu.make_async_remote_copy(
            src_ref=src,
            dst_ref=dst,
            send_sem=send,
            recv_sem=recv,
            device_id=device_at(z + dz % NZ, x + dx % NX, y + dy % NY, c + dc),
            device_id_type=MESH,
        )

    phrase_copy = pltpu.make_async_copy(phrase_hbm, raw, in_sem.at[0])
    phrase_copy.start()
    limits_copy = pltpu.make_async_copy(limits_hbm, limits_ref, in_sem.at[2])
    limits_copy.start()
    shard_copy = pltpu.make_async_copy(shard_hbm, flat_ref, in_sem.at[3])
    shard_copy.start()
    feature_copies = []
    for i in range(n_feature):
        rows = pl.ds(i * chunk, chunk)
        copy = pltpu.make_async_copy(feature_hbm.at[rows], feature.at[rows], feature_sem.at[i])
        copy.start()
        feature_copies.append(copy)
    sharp_copy = pltpu.make_async_copy(sharp_hbm, sharp_ref, in_sem.at[6])
    sharp_copy.start()
    shift_copy = pltpu.make_async_copy(shift_hbm, shift_ref, in_sem.at[7])
    shift_copy.start()
    named_copy = pltpu.make_async_copy(named_hbm.at[pl.ds(shard * 24, 24)], named, in_sem.at[1])
    named_copy.start()

    barrier = pltpu.get_barrier_semaphore()
    partners = [(dz, 0, 0, dc) for dz in range(NZ) for dc in range(2) if (dz, dc) != (0, 0)]
    partners += [(0, dx, 0, 0) for dx in range(1, NX)] + [(0, 0, 1, 0), (0, 0, 3, 0)]
    for dz, dx, dy, dc in partners:
        pl.semaphore_signal(
            barrier, inc=1, device_id=device_at(z + dz, x + dx, y + dy, c + dc), device_id_type=MESH
        )

    phrase_copy.wait()
    for i in range(0, ph_dev, 64):
        rows = pl.ds(i, 64)
        own = raw[rows].astype(F32)
        scale = lax.rsqrt(jnp.sum(own * own, axis=1, keepdims=True) + EPS)
        phrases[rows] = (own * scale).astype(BF16)
    shard_copy.wait()
    groups = n_dev // 4
    wide = jnp.concatenate([flat_ref[pl.ds(i, groups, stride=3), :] for i in range(3)], axis=1)
    for i in range(4):
        shard_ref[pl.ds(i * groups, groups)] = wide[:, i * reg_dev : (i + 1) * reg_dev]

    def shard_row(device):
        return (device & 3) * groups + (device >> 2)

    own = shard_ref[pl.ds(shard_row(me_img * 8 + me_phr), 1), :]
    member = (iota((32, reg_dev), 0) == own).astype(F32)
    earlier = (iota((reg_dev, reg_dev), 0) < iota((reg_dev, reg_dev), 1)).astype(BF16)
    rank = jnp.sum(member * dot(member.astype(BF16), earlier), axis=0, keepdims=True).astype(I32)
    parity = lax.rem(x, 2)
    to_z = ((own >> 2) - z + NZ) & (NZ - 1)
    to_c = jnp.where((own & 1) == c, 0, 1)
    to_x = jnp.where(((own >> 1) & 1) == parity, 0, 1)
    goes = ((to_z * 2 + to_c) * 2 + to_x) * SLOT + rank
    slots = NZ * 4 * SLOT
    dispatch = (iota((slots, reg_dev), 0) == goes).astype(BF16)

    limits_copy.wait()
    same = iota((reg_dev, reg_dev), 0) == iota((reg_dev, reg_dev), 1)

    def as_column(row):
        return jnp.sum(jnp.where(same, row.astype(F32), 0.0), axis=1, keepdims=True).astype(I32)

    limit = [limits_ref[j : j + 1, :] for j in range(4)]
    limit_column = [as_column(row) for row in limit]
    spot = iota((reg_dev, patches), 1)
    spot_row, spot_col = spot >> 4, spot & 15
    inside = (
        (spot_row >= limit_column[0])
        & (spot_row < limit_column[1])
        & (spot_col >= limit_column[2])
        & (spot_col < limit_column[3])
    )
    region = iota((reg_dev, patches), 0)
    images = chunk // patches

    def pool_chunk(i):
        feature_copies[i].wait()
        mask = jnp.concatenate(
            [
                (
                    inside
                    & (region >= (i * images + m) * reg_img)
                    & (region < (i * images + m + 1) * reg_img)
                ).astype(F32)
                for m in range(images)
            ],
            axis=1,
        ).astype(BF16)
        term = dot(mask, feature[pl.ds(i * chunk, chunk)])
        pool[...] = term if i == 0 else pool[...] + term

    for i in range(POOL_EARLY):
        pool_chunk(i)
    pl.semaphore_wait(barrier, len(partners))

    def ring(index, block, to_block, first, count, dy):
        return remote(
            phrases.at[pl.ds(block * ph_dev + first, count)],
            phrases.at[pl.ds(to_block * ph_dev + first, count)],
            y_send.at[index],
            y_recv.at[index],
            dy=dy,
        )

    ring_copies = [
        ring(0, 0, 1, 0, half, 1),
        ring(1, 0, 2, half, half, -1),
        ring(2, 0, 1, half, half, 1),
        ring(3, 0, 2, 0, half, -1),
        ring(4, 1, 3, 0, LANES, 1),
        ring(5, 2, 3, ph_dev - LANES, LANES, -1),
        ring(6, 1, 3, LANES, half - LANES, 1),
        ring(7, 2, 3, half, half - LANES, -1),
    ]
    for copy in ring_copies[: 2 if LATE_OWN else 4]:
        copy.start()

    for i in range(POOL_EARLY, n_feature):
        pool_chunk(i)
    z_out[...] = fold(dot(dispatch, pool[...].astype(BF16))).astype(BF16)

    def block(ref, index):
        return ref.at[pl.ds(index * 2 * SLOT, 2 * SLOT)]

    z_copies = {}
    for dz in ISSUE:
        for dc in range(2):
            if (dz, dc) == (0, 0):
                continue
            there = (NZ - dz) % NZ
            copy = remote(
                block(z_out, dz * 2 + dc),
                block(z_in, there * 2 + dc),
                zf_send.at[dz, dc],
                zf_recv.at[there, dc],
                dz=dz,
                dc=dc,
            )
            copy.start()
            z_copies[dz, dc] = copy

    live = 4 * NZ * 2 * SLOT
    member_all = (shard_ref[...] == shard).astype(BF16)
    rank_all = dot(member_all, earlier).astype(BF16)
    slot = iota((live, n_dev), 0)
    k, xr, dc_, r_ = slot >> 6, (slot >> 4) & 3, (slot >> 3) & 1, slot & 7
    rel = jnp.zeros_like(k)
    for rel_z, at in PLACE.items():
        rel = jnp.where(k == at, rel_z, rel)
    from_z = (z + rel) & (NZ - 1)
    from_x = (x + xr) & (NX - 1)
    from_c = (c + dc_) & 1
    device = ((from_z * 2 + (from_x & 1)) * 2 + from_c) * 8 + (from_x >> 1) * 4 + y
    pick = (iota((live, n_dev), 1) == shard_row(device)).astype(BF16)
    member_slot = dot(pick, member_all)
    rank_slot = dot(pick, rank_all)
    wanted = r_[:, :reg_dev].astype(F32)
    local = (iota((live, reg_dev), 1) + 1).astype(F32)
    held = jnp.sum(
        jnp.where(rank_slot == wanted, member_slot * local, 0.0), axis=1, keepdims=True
    ).astype(I32)
    ids[...] = jnp.where(held > 0, device[:, :128] * reg_dev + held - 1, -1)

    collect = (iota((reg_dev, slots), 1) == as_column(goes)).astype(BF16)
    spot = iota((patches, reg_dev), 0)
    spot_row, spot_col = spot >> 4, spot & 15
    inside = (
        (spot_row >= limit[0])
        & (spot_row < limit[1])
        & (spot_col >= limit[2])
        & (spot_col < limit[3])
    )
    region = iota((patches, reg_dev), 1)
    for m in range(reg_dev // reg_img):
        mask = (inside & (region >= m * reg_img) & (region < (m + 1) * reg_img)).astype(BF16)
        spread[pl.ds(m * patches, patches)] = dot(mask, collect).astype(BF16)
    spread_copy = pltpu.make_async_copy(spread, spread_hbm, in_sem.at[4])
    spread_copy.start()

    x_copies = {}
    for step, rel in enumerate(NEAR):
        at = PLACE[rel]
        if LATE_OWN and step == LATE_OWN:
            ring_copies[2].start()
            ring_copies[3].start()
        if step == LATE_PASS:
            ring_copies[0].wait_recv()
            ring_copies[4].start()
            ring_copies[1].wait_recv()
            ring_copies[5].start()
        if step == LATE_REST:
            ring_copies[6].start()
            ring_copies[7].start()
        sides = []
        for dc in range(2):
            if (rel, dc) == (0, 0):
                got = block(z_out, 0)
            else:
                got = block(z_in, rel * 2 + dc)
                z_copies[(NZ - rel) % NZ, dc].wait_recv()
            sides.append(got[...].astype(F32))
        near, far = [
            jnp.concatenate(
                [side[p * SLOT : (p + 1) * SLOT] for side in sides], axis=0
            ).astype(BF16)
            for p in range(2)
        ]
        block(x_in, at * 4)[...] = near
        block(x_out, rel * 2)[...] = near
        block(x_out, rel * 2 + 1)[...] = far
        for dx in (2, 1, 3):
            there = NX - dx
            copy = remote(
                block(x_out, rel * 2 + dx % 2),
                block(x_in, at * 4 + there),
                xf_send.at[rel, dx - 1],
                xf_recv.at[rel, there - 1],
                dx=dx,
            )
            copy.start()
            x_copies[rel, dx] = copy

    named_copy.wait()
    sharp_copy.wait()
    shift_copy.wait()
    sharp, shift = sharp_ref[0], shift_ref[0]
    for rel in NEAR:
        for dx in (2, 1, 3):
            x_copies[rel, dx].wait_recv()
        rows = pl.ds(PLACE[rel] * 64, 64)
        folded = x_in[rows].astype(F32)
        arrived = jnp.concatenate([folded, folded_columns(folded)], axis=1)
        inv = lax.rsqrt(jnp.sum(arrived * arrived, axis=1, keepdims=True) + EPS)
        regions[rows] = arrived.astype(BF16)
        inverse[rows] = jnp.broadcast_to(inv, (64, LANES))
        unit[rows] = (arrived * inv).astype(BF16)

    def pairs(rows, which, first, count, dy):
        them = phrases[pl.ds(which * ph_dev + first, count)]
        scores = lax.dot_general(
            unit[rows], them, (((1,), (1,)), ((), ())), preferred_element_type=F32
        )
        row = (me_phr // 4) * 12 + lax.rem(y + dy, NY) * 3 + first // LANES
        mine = ids[rows]
        weights = []
        for j in range(count // LANES):
            logits = sharp * scores[:, j * LANES : (j + 1) * LANES] + shift
            positive = (mine == named[pl.ds(row + j, 1), :]).astype(F32)
            weights.append((jax.nn.sigmoid(logits) - positive).astype(BF16))
        return dot(jnp.concatenate(weights, axis=1), them)

    everything = pl.ds(0, live)
    total[...] = pairs(everything, 0, 0, ph_dev, 0)
    ring_copies[2].wait_recv()
    total[...] += pairs(everything, 1, 0, ph_dev, 3)
    ring_copies[3].wait_recv()
    total[...] += pairs(everything, 2, 0, ph_dev, 1)
    ring_copies[4].wait_recv()
    total[...] += pairs(everything, 3, 0, LANES, 2)
    ring_copies[5].wait_recv()
    total[...] += pairs(everything, 3, ph_dev - LANES, LANES, 2)
    ring_copies[6].wait_recv()
    ring_copies[7].wait_recv()
    r_copies = {}
    for part in range(2):
        rows = pl.ds(part * (live // 2), live // 2)
        total[rows] += pairs(rows, 3, LANES, LANES, 2)
        for at in range(part * 4, part * 4 + 4):
            rows = pl.ds(at * 64, 64)
            pull = sharp * total[rows]
            arrived = regions[rows].astype(F32)
            inv = inverse[rows][:, 0:1]
            radial = jnp.sum(arrived * pull, axis=1, keepdims=True)
            p_out[rows] = fold(inv * pull - (inv * inv * inv * radial) * arrived).astype(BF16)
            for dx in (2, 1, 3):
                there = NX - dx
                copy = remote(
                    block(p_out, at * 4 + dx),
                    block(p_in, at * 4 + there),
                    xr_send.at[at, dx - 1],
                    xr_recv.at[at, there - 1],
                    dx=dx,
                )
                copy.start()
                r_copies[at, dx] = copy

    home_copies = {}
    for at, rel in enumerate(ORDER):
        for dx in (2, 1, 3):
            r_copies[at, dx].wait_recv()
        near = block(p_out, at * 4)[...].astype(F32) + block(p_in, at * 4 + 2)[...].astype(F32)
        far = block(p_in, at * 4 + 1)[...].astype(F32) + block(p_in, at * 4 + 3)[...].astype(F32)
        there = (NZ - rel) % NZ
        for dc in range(2):
            rows = slice(dc * SLOT, (dc + 1) * SLOT)
            block(s_out, at * 2 + dc)[...] = jnp.concatenate(
                [near[rows], far[rows]], axis=0
            ).astype(BF16)
            if (rel, dc) == (0, 0):
                stay = pltpu.make_async_copy(block(s_out, at * 2), block(back_hbm, 0), in_sem.at[5])
                stay.start()
                continue
            copy = remote(
                block(s_out, at * 2 + dc),
                block(back_hbm, there * 2 + dc),
                zr_send.at[rel, dc],
                zr_recv.at[there, dc],
                dz=rel,
                dc=dc,
            )
            copy.start()
            home_copies[rel, dc] = copy

    for copy in home_copies.values():
        copy.wait_recv()
    stay.wait()
    spread_copy.wait()
    for copies in (ring_copies, z_copies.values(), x_copies.values(), r_copies.values(), home_copies.values()):
        for copy in copies:
            copy.wait_send()


def spread_kernel(spread_hbm, back_hbm, out_hbm, spread, back, last, staged, in_sems, out_sems):
    keep = back.shape[1]
    n_chunk = out_sems.shape[0]
    rows = spread.shape[0] // n_chunk
    loads, stores = [], []
    back_copy = pltpu.make_async_copy(back_hbm, back, in_sems.at[n_chunk])
    back_copy.start()
    for i in range(n_chunk):
        part = pl.ds(i * rows, rows)
        loads.append(pltpu.make_async_copy(spread_hbm.at[part], spread.at[part], in_sems.at[i]))
        loads[i].start()
    back_copy.wait()
    last[...] = folded_columns(back[...].astype(F32)).astype(BF16)
    for i in range(n_chunk):
        part = pl.ds(i * rows, rows)
        loads[i].wait()
        staged[part, pl.ds(0, keep)] = dot(spread[part], back[...]).astype(BF16)
        staged[part, pl.ds(keep, LANES)] = dot(spread[part], last[...]).astype(BF16)
        stores.append(pltpu.make_async_copy(staged.at[part], out_hbm.at[part], out_sems.at[i]))
        stores[i].start()
    for copy in stores:
        copy.wait()


def shards(features, limits, shard_index, named, phrases, sharpness, shift):
    images, patches, width = features.shape
    reg_dev, ph_dev = limits.shape[0], phrases.shape[0]
    n_dev = shard_index.shape[0] // reg_dev
    slots = NZ * 4 * SLOT
    live = slots * 2
    keep = width - LANES
    hbm = pl.BlockSpec(memory_space=pltpu.HBM)
    dma = pltpu.SemaphoreType.DMA
    back, spread = pl.pallas_call(
        exchange_kernel,
        out_shape=(
            jax.ShapeDtypeStruct((slots, keep), BF16),
            jax.ShapeDtypeStruct((images * patches, slots), BF16),
        ),
        in_specs=[hbm] * 7,
        out_specs=(hbm, hbm),
        scratch_shapes=[
            pltpu.VMEM((images * patches, width), BF16),
            pltpu.VMEM((ph_dev, width), BF16),
            pltpu.VMEM((24, LANES), I32),
            pltpu.SMEM((1,), F32),
            pltpu.SMEM((1,), F32),
            pltpu.VMEM((4, reg_dev), I32),
            pltpu.VMEM((n_dev * reg_dev // LANES, LANES), I32),
            pltpu.VMEM((n_dev, reg_dev), I32),
            pltpu.VMEM((NY * ph_dev, width), BF16),
            pltpu.VMEM((reg_dev, width), F32),
            pltpu.VMEM((slots, keep), BF16),
            pltpu.VMEM((slots, keep), BF16),
            pltpu.VMEM((slots, keep), BF16),
            pltpu.VMEM((live, keep), BF16),
            pltpu.VMEM((live, width), BF16),
            pltpu.VMEM((live, width), BF16),
            pltpu.VMEM((live, LANES), I32),
            pltpu.VMEM((live, LANES), F32),
            pltpu.VMEM((live, width), F32),
            pltpu.VMEM((live, keep), BF16),
            pltpu.VMEM((live, keep), BF16),
            pltpu.VMEM((slots, keep), BF16),
            pltpu.VMEM((images * patches, slots), BF16),
            dma((8,)),
            dma((4,)),
            dma((8,)),
            dma((8,)),
            dma((NZ, 2)),
            dma((NZ, 2)),
            dma((NZ, 3)),
            dma((NZ, 3)),
            dma((NZ, 3)),
            dma((NZ, 3)),
            dma((NZ, 2)),
            dma((NZ, 2)),
        ],
        compiler_params=pltpu.CompilerParams(
            collective_id=0, has_side_effects=True, vmem_limit_bytes=62 * 2**20
        ),
    )(
        sharpness,
        shift,
        limits.T,
        shard_index.reshape(-1, 128),
        named.reshape(-1, 128),
        phrases,
        features.reshape(images * patches, width),
    )
    out = pl.pallas_call(
        spread_kernel,
        out_shape=jax.ShapeDtypeStruct((images * patches, width), BF16),
        in_specs=[hbm, hbm],
        out_specs=hbm,
        scratch_shapes=[
            pltpu.VMEM((images * patches, slots), BF16),
            pltpu.VMEM((slots, keep), BF16),
            pltpu.VMEM((slots, LANES), BF16),
            pltpu.VMEM((images * patches, width), BF16),
            dma((9,)),
            dma((8,)),
        ],
        compiler_params=pltpu.CompilerParams(vmem_limit_bytes=62 * 2**20),
    )(spread, back)
    return out.reshape(images, patches, width)


def solution(mesh):
    return jax.shard_map(
        shards,
        mesh=mesh,
        in_specs=(
            P(("img", "phr"), None, None),
            P(("img", "phr"), None),
            P(),
            P(),
            P(("img", "phr"), None),
            P(),
            P(),
        ),
        out_specs=P(("img", "phr"), None, None),
        check_vma=False,
    )
```

```python
import jax
import jax.numpy as jnp
from jax import lax
from jax.experimental import pallas as pl
from jax.experimental.pallas import tpu as pltpu
from jax.sharding import PartitionSpec as P

MESH = pl.DeviceIdType.MESH
GRID = 16
NZ, NX, NY = 8, 4, 4
SLOT = 8
EPS = 1e-06
BF16, F32, I32 = jnp.bfloat16, jnp.float32, jnp.int32

ORDER = (4, 3, 5, 2, 6, 1, 7, 0)
PLACE = {rel: k for k, rel in enumerate(ORDER)}
NEAR = (0, 1, 7, 6, 2, 5, 3, 4)
ISSUE = NEAR
PARTS = ((0, 2), (2, 4), (4, 8))
LATE_OWN = 1
LATE_PASS = 5
LATE_REST = 7
LANES = 128


def place():
    img, phr = lax.axis_index("img"), lax.axis_index("phr")
    return img // 4, (phr // 4) * 2 + (img // 2) % 2, phr % 4, img % 2


def device_at(z, x, y, c):
    z, x, y, c = lax.rem(z, NZ), lax.rem(x, NX), lax.rem(y, NY), lax.rem(c, 2)
    return ((z * 2 + lax.rem(x, 2)) * 2 + c, (x // 2) * 4 + y)


def iota(shape, dim):
    return lax.broadcasted_iota(I32, shape, dim)


def dot(a, b):
    return jnp.dot(a, b, preferred_element_type=F32)


def fold(value):
    groups, keep = value.shape[0] // SLOT, value.shape[1] - LANES
    value = value.reshape(groups, SLOT, keep + LANES)
    tiles = [value[:, t : t + 1, keep:] for t in range(SLOT - 1)]
    tiles.append(jnp.zeros((groups, 1, keep - (SLOT - 1) * LANES), F32))
    spare = iota((groups, SLOT, keep), 1) == SLOT - 1
    folded = jnp.where(spare, jnp.concatenate(tiles, axis=2), value[:, :, :keep])
    return folded.reshape(groups * SLOT, keep)


def folded_columns(folded):
    groups, keep = folded.shape[0] // SLOT, folded.shape[1]
    folded = folded.reshape(groups, SLOT, keep)
    row = iota((groups, SLOT, LANES), 1)
    columns = jnp.zeros((groups, SLOT, LANES), F32)
    for t in range(SLOT - 1):
        tile = folded[:, SLOT - 1 : SLOT, t * LANES : (t + 1) * LANES]
        columns = jnp.where(row == t, tile, columns)
    return columns.reshape(groups * SLOT, LANES)


def exchange_kernel(
    sharp_hbm,
    shift_hbm,
    limits_hbm,
    shard_hbm,
    named_hbm,
    phrase_hbm,
    feature_hbm,
    back_hbm,
    spread_hbm,
    feature,
    raw,
    named,
    sharp_ref,
    shift_ref,
    limits_ref,
    flat_ref,
    shard_ref,
    ring_in,
    phrases,
    pool,
    z_out,
    z_in,
    x_out,
    x_in,
    regions,
    unit,
    ids,
    inverse,
    total,
    p_out,
    p_in,
    s_out,
    spread,
    in_sem,
    feature_sem,
    y_send,
    y_recv,
    zf_send,
    zf_recv,
    xf_send,
    xf_recv,
    xr_send,
    xr_recv,
    zr_send,
    zr_recv,
    ready,
):
    z, x, y, c = place()
    me_img, me_phr = lax.axis_index("img"), lax.axis_index("phr")
    shard = me_img
    reg_dev = limits_ref.shape[1]
    n_dev = shard_ref.shape[0]
    ph_dev = raw.shape[0]
    half = ph_dev // 2
    reg_img = 12
    patches = GRID * GRID
    n_feature = feature_sem.shape[0]
    chunk = feature.shape[0] // n_feature

    def remote(src, dst, send, recv, dz=0, dx=0, dy=0, dc=0):
        return pltpu.make_async_remote_copy(
            src_ref=src,
            dst_ref=dst,
            send_sem=send,
            recv_sem=recv,
            device_id=device_at(z + dz % NZ, x + dx % NX, y + dy % NY, c + dc),
            device_id_type=MESH,
        )

    limits_copy = pltpu.make_async_copy(limits_hbm, limits_ref, in_sem.at[2])
    limits_copy.start()
    shard_copy = pltpu.make_async_copy(shard_hbm, flat_ref, in_sem.at[3])
    shard_copy.start()
    feature_copies = []
    for i in range(n_feature):
        rows = pl.ds(i * chunk, chunk)
        copy = pltpu.make_async_copy(feature_hbm.at[rows], feature.at[rows], feature_sem.at[i])
        copy.start()
        feature_copies.append(copy)
    sharp_copy = pltpu.make_async_copy(sharp_hbm, sharp_ref, in_sem.at[6])
    sharp_copy.start()
    shift_copy = pltpu.make_async_copy(shift_hbm, shift_ref, in_sem.at[7])
    shift_copy.start()
    phrase_copy = pltpu.make_async_copy(phrase_hbm, raw, in_sem.at[0])
    phrase_copy.start()
    named_copy = pltpu.make_async_copy(named_hbm.at[pl.ds(shard * 24, 24)], named, in_sem.at[1])
    named_copy.start()

    def tell(semaphore, partners):
        for dz, dx, dy, dc in partners:
            pl.semaphore_signal(
                semaphore,
                inc=1,
                device_id=device_at(z + dz, x + dx, y + dy, c + dc),
                device_id_type=MESH,
            )

    barrier = pltpu.get_barrier_semaphore()
    along_x, along_y = [(0, 1, 0, 0), (0, 3, 0, 0)], [(0, 0, 1, 0), (0, 0, 3, 0)]
    along_z = [(1, 0, 0, 0), (7, 0, 0, 0)]
    neighbours = along_y + [(0, 0, 0, 1)] + along_x + along_z
    tell(barrier, neighbours)
    pl.semaphore_wait(barrier, len(neighbours))

    def ring(index, block, to_block, first, count, dy):
        source = phrase_hbm if block == 0 else ring_in
        return remote(
            source.at[pl.ds(max(block - 1, 0) * ph_dev + first, count)],
            ring_in.at[pl.ds((to_block - 1) * ph_dev + first, count)],
            y_send.at[index],
            y_recv.at[index],
            dy=dy,
        )

    ring_copies = [
        ring(0, 0, 1, 0, half, 1),
        ring(1, 0, 2, half, half, -1),
        ring(2, 0, 1, half, half, 1),
        ring(3, 0, 2, 0, half, -1),
        ring(4, 1, 3, 0, LANES, 1),
        ring(5, 2, 3, ph_dev - LANES, LANES, -1),
        ring(6, 1, 3, LANES, half - LANES, 1),
        ring(7, 2, 3, half, half - LANES, -1),
    ]
    for copy in ring_copies[: 2 if LATE_OWN else 4]:
        copy.start()

    tell(ready.at[0], along_x)
    tell(ready.at[1], along_z)

    def hear(step):
        pl.semaphore_wait(ready.at[step], 2)
        if step < 4:
            tell(ready.at[step + 1], along_z)

    shard_copy.wait()
    groups = n_dev // 4
    wide = jnp.concatenate([flat_ref[pl.ds(i, groups, stride=3), :] for i in range(3)], axis=1)
    for i in range(4):
        shard_ref[pl.ds(i * groups, groups)] = wide[:, i * reg_dev : (i + 1) * reg_dev]

    def shard_row(device):
        return (device & 3) * groups + (device >> 2)

    own = shard_ref[pl.ds(shard_row(me_img * 8 + me_phr), 1), :]
    member = (iota((32, reg_dev), 0) == own).astype(F32)
    earlier = (iota((reg_dev, reg_dev), 0) < iota((reg_dev, reg_dev), 1)).astype(BF16)
    rank = jnp.sum(member * dot(member.astype(BF16), earlier), axis=0, keepdims=True).astype(I32)
    parity = lax.rem(x, 2)
    to_z = ((own >> 2) - z + NZ) & (NZ - 1)
    to_c = jnp.where((own & 1) == c, 0, 1)
    to_x = jnp.where(((own >> 1) & 1) == parity, 0, 1)
    goes = ((to_z * 2 + to_c) * 2 + to_x) * SLOT + rank
    slots = NZ * 4 * SLOT
    dispatch = (iota((slots, reg_dev), 0) == goes).astype(BF16)

    limits_copy.wait()
    same = iota((reg_dev, reg_dev), 0) == iota((reg_dev, reg_dev), 1)

    def as_column(row):
        return jnp.sum(jnp.where(same, row.astype(F32), 0.0), axis=1, keepdims=True).astype(I32)

    limit = [limits_ref[j : j + 1, :] for j in range(4)]
    limit_column = [as_column(row) for row in limit]
    spot = iota((reg_dev, patches), 1)
    spot_row, spot_col = spot >> 4, spot & 15
    inside = (
        (spot_row >= limit_column[0])
        & (spot_row < limit_column[1])
        & (spot_col >= limit_column[2])
        & (spot_col < limit_column[3])
    )
    region = iota((reg_dev, patches), 0)
    images = chunk // patches

    def pool_chunk(i):
        feature_copies[i].wait()
        mask = jnp.concatenate(
            [
                (
                    inside
                    & (region >= (i * images + m) * reg_img)
                    & (region < (i * images + m + 1) * reg_img)
                ).astype(F32)
                for m in range(images)
            ],
            axis=1,
        ).astype(BF16)
        term = dot(mask, feature[pl.ds(i * chunk, chunk)])
        pool[...] = term if i == 0 else pool[...] + term

    for i in range(n_feature):
        pool_chunk(i)
        hear(i + 1)
    pl.semaphore_wait(ready.at[0], 2)
    z_out[...] = fold(dot(dispatch, pool[...].astype(BF16))).astype(BF16)

    def block(ref, index):
        return ref.at[pl.ds(index * 2 * SLOT, 2 * SLOT)]

    z_copies = {}
    for dz in ISSUE:
        for dc in range(2):
            if (dz, dc) == (0, 0):
                continue
            there = (NZ - dz) % NZ
            copy = remote(
                block(z_out, dz * 2 + dc),
                block(z_in, there * 2 + dc),
                zf_send.at[dz, dc],
                zf_recv.at[there, dc],
                dz=dz,
                dc=dc,
            )
            copy.start()
            z_copies[dz, dc] = copy

    def to_unit(source, block, first, count):
        for i in range(first, first + count, 64):
            rows = pl.ds(max(block - 1, 0) * ph_dev + i, 64)
            them = source[rows].astype(F32)
            scale = lax.rsqrt(jnp.sum(them * them, axis=1, keepdims=True) + EPS)
            phrases[pl.ds(block * ph_dev + i, 64)] = (them * scale).astype(BF16)

    phrase_copy.wait()
    to_unit(raw, 0, 0, ph_dev)

    live = 4 * NZ * 2 * SLOT
    member_all = (shard_ref[...] == shard).astype(BF16)
    rank_all = dot(member_all, earlier).astype(BF16)
    slot = iota((live, n_dev), 0)
    k, xr, dc_, r_ = slot >> 6, (slot >> 4) & 3, (slot >> 3) & 1, slot & 7
    rel = jnp.zeros_like(k)
    for rel_z, at in PLACE.items():
        rel = jnp.where(k == at, rel_z, rel)
    from_z = (z + rel) & (NZ - 1)
    from_x = (x + xr) & (NX - 1)
    from_c = (c + dc_) & 1
    device = ((from_z * 2 + (from_x & 1)) * 2 + from_c) * 8 + (from_x >> 1) * 4 + y
    pick = (iota((live, n_dev), 1) == shard_row(device)).astype(BF16)
    member_slot = dot(pick, member_all)
    rank_slot = dot(pick, rank_all)
    wanted = r_[:, :reg_dev].astype(F32)
    local = (iota((live, reg_dev), 1) + 1).astype(F32)
    held = jnp.sum(
        jnp.where(rank_slot == wanted, member_slot * local, 0.0), axis=1, keepdims=True
    ).astype(I32)
    ids[...] = jnp.where(held > 0, device[:, :128] * reg_dev + held - 1, -1)

    collect = (iota((reg_dev, slots), 1) == as_column(goes)).astype(BF16)
    spot = iota((patches, reg_dev), 0)
    spot_row, spot_col = spot >> 4, spot & 15
    inside = (
        (spot_row >= limit[0])
        & (spot_row < limit[1])
        & (spot_col >= limit[2])
        & (spot_col < limit[3])
    )
    region = iota((patches, reg_dev), 1)
    for m in range(reg_dev // reg_img):
        mask = (inside & (region >= m * reg_img) & (region < (m + 1) * reg_img)).astype(BF16)
        spread[pl.ds(m * patches, patches)] = dot(mask, collect).astype(BF16)
    spread_copy = pltpu.make_async_copy(spread, spread_hbm, in_sem.at[4])
    spread_copy.start()

    x_copies = {}
    for step, rel in enumerate(NEAR):
        at = PLACE[rel]
        if LATE_OWN and step == LATE_OWN:
            ring_copies[2].start()
            ring_copies[3].start()
        if step == LATE_PASS:
            ring_copies[0].wait_recv()
            ring_copies[4].start()
            ring_copies[1].wait_recv()
            ring_copies[5].start()
        if step == LATE_REST:
            ring_copies[6].start()
            ring_copies[7].start()
        sides = []
        for dc in range(2):
            if (rel, dc) == (0, 0):
                got = block(z_out, 0)
            else:
                got = block(z_in, rel * 2 + dc)
                z_copies[(NZ - rel) % NZ, dc].wait_recv()
            sides.append(got[...].astype(F32))
        near, far = [
            jnp.concatenate(
                [side[p * SLOT : (p + 1) * SLOT] for side in sides], axis=0
            ).astype(BF16)
            for p in range(2)
        ]
        block(x_in, at * 4)[...] = near
        block(x_out, rel * 2)[...] = near
        block(x_out, rel * 2 + 1)[...] = far
        for dx in (2, 1, 3):
            there = NX - dx
            copy = remote(
                block(x_out, rel * 2 + dx % 2),
                block(x_in, at * 4 + there),
                xf_send.at[rel, dx - 1],
                xf_recv.at[rel, there - 1],
                dx=dx,
            )
            copy.start()
            x_copies[rel, dx] = copy

    named_copy.wait()
    sharp_copy.wait()
    shift_copy.wait()
    sharp, shift = sharp_ref[0], shift_ref[0]

    def arrive(rel):
        for dx in (2, 1, 3):
            x_copies[rel, dx].wait_recv()
        rows = pl.ds(PLACE[rel] * 64, 64)
        folded = x_in[rows].astype(F32)
        arrived = jnp.concatenate([folded, folded_columns(folded)], axis=1)
        inv = lax.rsqrt(jnp.sum(arrived * arrived, axis=1, keepdims=True) + EPS)
        regions[rows] = arrived.astype(BF16)
        inverse[rows] = jnp.broadcast_to(inv, (64, LANES))
        unit[rows] = (arrived * inv).astype(BF16)

    def pairs(rows, first, count):
        them = phrases[pl.ds(first, count)]
        scores = lax.dot_general(
            unit[rows], them, (((1,), (1,)), ((), ())), preferred_element_type=F32
        )
        mine = ids[rows]
        weights = []
        for j in range(count // LANES):
            block, inner = divmod(first + j * LANES, ph_dev)
            row = (me_phr // 4) * 12 + lax.rem(y + (0, 3, 1, 2)[block], NY) * 3 + inner // LANES
            logits = sharp * scores[:, j * LANES : (j + 1) * LANES] + shift
            positive = (mine == named[pl.ds(row, 1), :]).astype(F32)
            weights.append((jax.nn.sigmoid(logits) - positive).astype(BF16))
        return dot(jnp.concatenate(weights, axis=1), them)

    everything, far_half, near_half = pl.ds(0, live), pl.ds(0, live // 2), pl.ds(live // 2, live // 2)
    for rel in NEAR[:4]:
        arrive(rel)
    ring_copies[2].wait_recv()
    to_unit(ring_in, 1, 0, ph_dev)
    total[near_half] = pairs(near_half, 0, 2 * ph_dev)
    for rel in NEAR[4:]:
        arrive(rel)
    total[far_half] = pairs(far_half, 0, 2 * ph_dev)
    ring_copies[3].wait_recv()
    to_unit(ring_in, 2, 0, ph_dev)
    ring_copies[4].wait_recv()
    to_unit(ring_in, 3, 0, LANES)
    total[...] += pairs(everything, 2 * ph_dev, ph_dev + LANES)
    ring_copies[5].wait_recv()
    to_unit(ring_in, 3, 2 * LANES, LANES)
    ring_copies[6].wait_recv()
    ring_copies[7].wait_recv()
    to_unit(ring_in, 3, LANES, LANES)
    r_copies = {}
    for begin, end in PARTS:
        rows = pl.ds(begin * 64, (end - begin) * 64)
        total[rows] += pairs(rows, 3 * ph_dev + LANES, 2 * LANES)
        for at in range(begin, end):
            rows = pl.ds(at * 64, 64)
            pull = sharp * total[rows]
            arrived = regions[rows].astype(F32)
            inv = inverse[rows][:, 0:1]
            radial = jnp.sum(arrived * pull, axis=1, keepdims=True)
            p_out[rows] = fold(inv * pull - (inv * inv * inv * radial) * arrived).astype(BF16)
            for dx in (2, 1, 3):
                there = NX - dx
                copy = remote(
                    block(p_out, at * 4 + dx),
                    block(p_in, at * 4 + there),
                    xr_send.at[at, dx - 1],
                    xr_recv.at[at, there - 1],
                    dx=dx,
                )
                copy.start()
                r_copies[at, dx] = copy

    home_copies = {}
    for at, rel in enumerate(ORDER):
        for dx in (2, 1, 3):
            r_copies[at, dx].wait_recv()
        near = block(p_out, at * 4)[...].astype(F32) + block(p_in, at * 4 + 2)[...].astype(F32)
        far = block(p_in, at * 4 + 1)[...].astype(F32) + block(p_in, at * 4 + 3)[...].astype(F32)
        there = (NZ - rel) % NZ
        for dc in range(2):
            rows = slice(dc * SLOT, (dc + 1) * SLOT)
            block(s_out, at * 2 + dc)[...] = jnp.concatenate(
                [near[rows], far[rows]], axis=0
            ).astype(BF16)
            if (rel, dc) == (0, 0):
                stay = pltpu.make_async_copy(block(s_out, at * 2), block(back_hbm, 0), in_sem.at[5])
                stay.start()
                continue
            copy = remote(
                block(s_out, at * 2 + dc),
                block(back_hbm, there * 2 + dc),
                zr_send.at[rel, dc],
                zr_recv.at[there, dc],
                dz=rel,
                dc=dc,
            )
            copy.start()
            home_copies[rel, dc] = copy

    for copy in home_copies.values():
        copy.wait_recv()
    stay.wait()
    spread_copy.wait()
    for copies in (ring_copies, z_copies.values(), x_copies.values(), r_copies.values(), home_copies.values()):
        for copy in copies:
            copy.wait_send()


def spread_kernel(spread_hbm, back_hbm, out_hbm, spread, back, last, staged, in_sems, out_sems):
    keep = back.shape[1]
    half = spread.shape[0] // 2
    back_copy = pltpu.make_async_copy(back_hbm, back, in_sems.at[2])
    back_copy.start()
    loads, stores = [], []
    for i in range(2):
        part = pl.ds(i * half, half)
        loads.append(pltpu.make_async_copy(spread_hbm.at[part], spread.at[part], in_sems.at[i]))
        loads[i].start()
    back_copy.wait()
    last[...] = folded_columns(back[...].astype(F32)).astype(BF16)
    for first in range(0, keep + LANES, 2 * LANES):
        columns = pl.ds(first, min(2 * LANES, keep + LANES - first))
        slots = back[:, columns] if first < keep else last[...]
        for i in range(2):
            if first == 0:
                loads[i].wait()
            part = pl.ds(i * half, half)
            staged[part, columns] = dot(spread[part], slots).astype(BF16)
        copy = pltpu.make_async_copy(
            staged.at[:, columns], out_hbm.at[:, columns], out_sems.at[len(stores)]
        )
        copy.start()
        stores.append(copy)
    for copy in stores:
        copy.wait()


def shards(features, limits, shard_index, named, phrases, sharpness, shift):
    images, patches, width = features.shape
    reg_dev, ph_dev = limits.shape[0], phrases.shape[0]
    n_dev = shard_index.shape[0] // reg_dev
    slots = NZ * 4 * SLOT
    live = slots * 2
    keep = width - LANES
    hbm = pl.BlockSpec(memory_space=pltpu.HBM)
    dma = pltpu.SemaphoreType.DMA
    back, spread = pl.pallas_call(
        exchange_kernel,
        out_shape=(
            jax.ShapeDtypeStruct((slots, keep), BF16),
            jax.ShapeDtypeStruct((images * patches, slots), BF16),
        ),
        in_specs=[hbm] * 7,
        out_specs=(hbm, hbm),
        scratch_shapes=[
            pltpu.VMEM((images * patches, width), BF16),
            pltpu.VMEM((ph_dev, width), BF16),
            pltpu.VMEM((24, LANES), I32),
            pltpu.SMEM((1,), F32),
            pltpu.SMEM((1,), F32),
            pltpu.VMEM((4, reg_dev), I32),
            pltpu.VMEM((n_dev * reg_dev // LANES, LANES), I32),
            pltpu.VMEM((n_dev, reg_dev), I32),
            pltpu.VMEM(((NY - 1) * ph_dev, width), BF16),
            pltpu.VMEM((NY * ph_dev, width), BF16),
            pltpu.VMEM((reg_dev, width), F32),
            pltpu.VMEM((slots, keep), BF16),
            pltpu.VMEM((slots, keep), BF16),
            pltpu.VMEM((slots, keep), BF16),
            pltpu.VMEM((live, keep), BF16),
            pltpu.VMEM((live, width), BF16),
            pltpu.VMEM((live, width), BF16),
            pltpu.VMEM((live, LANES), I32),
            pltpu.VMEM((live, LANES), F32),
            pltpu.VMEM((live, width), F32),
            pltpu.VMEM((live, keep), BF16),
            pltpu.VMEM((live, keep), BF16),
            pltpu.VMEM((slots, keep), BF16),
            pltpu.VMEM((images * patches, slots), BF16),
            dma((8,)),
            dma((4,)),
            dma((8,)),
            dma((8,)),
            dma((NZ, 2)),
            dma((NZ, 2)),
            dma((NZ, 3)),
            dma((NZ, 3)),
            dma((NZ, 3)),
            dma((NZ, 3)),
            dma((NZ, 2)),
            dma((NZ, 2)),
            pltpu.SemaphoreType.REGULAR((5,)),
        ],
        compiler_params=pltpu.CompilerParams(
            collective_id=0, has_side_effects=True, vmem_limit_bytes=62 * 2**20
        ),
    )(
        sharpness,
        shift,
        limits.T,
        shard_index.reshape(-1, 128),
        named.reshape(-1, 128),
        phrases,
        features.reshape(images * patches, width),
    )
    out = pl.pallas_call(
        spread_kernel,
        out_shape=jax.ShapeDtypeStruct((images * patches, width), BF16),
        in_specs=[hbm, hbm],
        out_specs=hbm,
        scratch_shapes=[
            pltpu.VMEM((images * patches, slots), BF16),
            pltpu.VMEM((slots, keep), BF16),
            pltpu.VMEM((slots, LANES), BF16),
            pltpu.VMEM((images * patches, width), BF16),
            dma((3,)),
            dma((width // LANES // 2 + 1,)),
        ],
        compiler_params=pltpu.CompilerParams(vmem_limit_bytes=62 * 2**20),
    )(spread, back)
    return out.reshape(images, patches, width)


def solution(mesh):
    return jax.shard_map(
        shards,
        mesh=mesh,
        in_specs=(
            P(("img", "phr"), None, None),
            P(("img", "phr"), None),
            P(),
            P(),
            P(("img", "phr"), None),
            P(),
            P(),
        ),
        out_specs=P(("img", "phr"), None, None),
        check_vma=False,
    )
```

```python
import jax
import jax.numpy as jnp
from jax import lax
from jax.experimental import pallas as pl
from jax.experimental.pallas import tpu as pltpu
from jax.sharding import PartitionSpec as P

MESH = pl.DeviceIdType.MESH
GRID = 16
NZ, NX, NY = 8, 4, 4
SLOT = 8
EPS = 1e-06
BF16, F32, I32 = jnp.bfloat16, jnp.float32, jnp.int32

ORDER = (4, 3, 5, 2, 6, 1, 7, 0)
PLACE = {rel: k for k, rel in enumerate(ORDER)}
NEAR = (0, 1, 7, 6, 2, 5, 3, 4)
ISSUE = NEAR
PARTS = ((0, 4), (4, 8))
LEAD = 4
LATE_OWN = 1
LATE_PASS = 3
LANES = 128


def place():
    img, phr = lax.axis_index("img"), lax.axis_index("phr")
    return img // 4, (phr // 4) * 2 + (img // 2) % 2, phr % 4, img % 2


def device_at(z, x, y, c):
    z, x, y, c = lax.rem(z, NZ), lax.rem(x, NX), lax.rem(y, NY), lax.rem(c, 2)
    return ((z * 2 + lax.rem(x, 2)) * 2 + c, (x // 2) * 4 + y)


def iota(shape, dim):
    return lax.broadcasted_iota(I32, shape, dim)


def dot(a, b):
    return jnp.dot(a, b, preferred_element_type=F32)


def fold(value):
    groups, keep = value.shape[0] // SLOT, value.shape[1] - LANES
    value = value.reshape(groups, SLOT, keep + LANES)
    tiles = [value[:, t : t + 1, keep:] for t in range(SLOT - 1)]
    tiles.append(jnp.zeros((groups, 1, keep - (SLOT - 1) * LANES), F32))
    spare = iota((groups, SLOT, keep), 1) == SLOT - 1
    folded = jnp.where(spare, jnp.concatenate(tiles, axis=2), value[:, :, :keep])
    return folded.reshape(groups * SLOT, keep)


def folded_columns(folded):
    groups, keep = folded.shape[0] // SLOT, folded.shape[1]
    folded = folded.reshape(groups, SLOT, keep)
    row = iota((groups, SLOT, LANES), 1)
    columns = jnp.zeros((groups, SLOT, LANES), F32)
    for t in range(SLOT - 1):
        tile = folded[:, SLOT - 1 : SLOT, t * LANES : (t + 1) * LANES]
        columns = jnp.where(row == t, tile, columns)
    return columns.reshape(groups * SLOT, LANES)


def exchange_kernel(
    sharp_hbm,
    shift_hbm,
    limits_hbm,
    shard_hbm,
    named_hbm,
    phrase_hbm,
    feature_hbm,
    back_hbm,
    spread_hbm,
    feature,
    raw,
    named,
    sharp_ref,
    shift_ref,
    limits_ref,
    flat_ref,
    shard_ref,
    ring_in,
    phrases,
    pool,
    z_out,
    z_in,
    x_out,
    x_in,
    regions,
    unit,
    ids,
    inverse,
    total,
    p_out,
    p_in,
    s_out,
    spread,
    in_sem,
    feature_sem,
    y_send,
    y_recv,
    zf_send,
    zf_recv,
    xf_send,
    xf_recv,
    xr_send,
    xr_recv,
    zr_send,
    zr_recv,
    ready,
):
    z, x, y, c = place()
    me_img, me_phr = lax.axis_index("img"), lax.axis_index("phr")
    shard = me_img
    reg_dev = limits_ref.shape[1]
    n_dev = shard_ref.shape[0]
    ph_dev = raw.shape[0]
    half = ph_dev // 2
    reg_img = 12
    patches = GRID * GRID
    n_feature = feature_sem.shape[0]
    chunk = feature.shape[0] // n_feature

    def remote(src, dst, send, recv, dz=0, dx=0, dy=0, dc=0):
        return pltpu.make_async_remote_copy(
            src_ref=src,
            dst_ref=dst,
            send_sem=send,
            recv_sem=recv,
            device_id=device_at(z + dz % NZ, x + dx % NX, y + dy % NY, c + dc),
            device_id_type=MESH,
        )

    limits_copy = pltpu.make_async_copy(limits_hbm, limits_ref, in_sem.at[2])
    limits_copy.start()
    shard_copy = pltpu.make_async_copy(shard_hbm, flat_ref, in_sem.at[3])
    shard_copy.start()
    feature_copies = []
    for i in range(n_feature):
        rows = pl.ds(i * chunk, chunk)
        copy = pltpu.make_async_copy(feature_hbm.at[rows], feature.at[rows], feature_sem.at[i])
        copy.start()
        feature_copies.append(copy)
    sharp_copy = pltpu.make_async_copy(sharp_hbm, sharp_ref, in_sem.at[6])
    sharp_copy.start()
    shift_copy = pltpu.make_async_copy(shift_hbm, shift_ref, in_sem.at[7])
    shift_copy.start()
    phrase_copy = pltpu.make_async_copy(phrase_hbm, raw, in_sem.at[0])
    phrase_copy.start()
    named_copy = pltpu.make_async_copy(named_hbm.at[pl.ds(shard * 24, 24)], named, in_sem.at[1])
    named_copy.start()

    def tell(semaphore, partners):
        for dz, dx, dy, dc in partners:
            pl.semaphore_signal(
                semaphore,
                inc=1,
                device_id=device_at(z + dz, x + dx, y + dy, c + dc),
                device_id_type=MESH,
            )

    barrier = pltpu.get_barrier_semaphore()
    along_x, along_y = [(0, 1, 0, 0), (0, 3, 0, 0)], [(0, 0, 1, 0), (0, 0, 3, 0)]
    along_z = [(1, 0, 0, 0), (7, 0, 0, 0)]
    neighbours = along_y + [(0, 0, 0, 1)] + along_x + along_z
    tell(barrier, neighbours)
    pl.semaphore_wait(barrier, len(neighbours))

    def ring(index, block, to_block, first, count, dy):
        source = phrase_hbm if block == 0 else ring_in
        return remote(
            source.at[pl.ds(max(block - 1, 0) * ph_dev + first, count)],
            ring_in.at[pl.ds((to_block - 1) * ph_dev + first, count)],
            y_send.at[index],
            y_recv.at[index],
            dy=dy,
        )

    ring_copies = [
        ring(0, 0, 1, 0, half, 1),
        ring(1, 0, 2, half, half, -1),
        ring(2, 0, 1, half, half, 1),
        ring(3, 0, 2, 0, half, -1),
        ring(4, 1, 3, 0, LANES, 1),
        ring(5, 2, 3, ph_dev - LANES, LANES, -1),
        ring(6, 1, 3, LANES, half - LANES, 1),
        ring(7, 2, 3, half, half - LANES, -1),
    ]
    for copy in ring_copies[:2]:
        copy.start()

    tell(ready.at[0], along_x)
    tell(ready.at[1], along_z)

    def hear(step):
        pl.semaphore_wait(ready.at[step], 2)
        if step < 4:
            tell(ready.at[step + 1], along_z)

    shard_copy.wait()
    groups = n_dev // 4
    wide = jnp.concatenate([flat_ref[pl.ds(i, groups, stride=3), :] for i in range(3)], axis=1)
    for i in range(4):
        shard_ref[pl.ds(i * groups, groups)] = wide[:, i * reg_dev : (i + 1) * reg_dev]

    def shard_row(device):
        return (device & 3) * groups + (device >> 2)

    own = shard_ref[pl.ds(shard_row(me_img * 8 + me_phr), 1), :]
    member = (iota((32, reg_dev), 0) == own).astype(F32)
    earlier = (iota((reg_dev, reg_dev), 0) < iota((reg_dev, reg_dev), 1)).astype(BF16)
    rank = jnp.sum(member * dot(member.astype(BF16), earlier), axis=0, keepdims=True).astype(I32)
    parity = lax.rem(x, 2)
    to_z = ((own >> 2) - z + NZ) & (NZ - 1)
    to_c = jnp.where((own & 1) == c, 0, 1)
    to_x = jnp.where(((own >> 1) & 1) == parity, 0, 1)
    goes = ((to_z * 2 + to_c) * 2 + to_x) * SLOT + rank
    slots = NZ * 4 * SLOT
    dispatch = (iota((slots, reg_dev), 0) == goes).astype(BF16)

    limits_copy.wait()
    same = iota((reg_dev, reg_dev), 0) == iota((reg_dev, reg_dev), 1)

    def as_column(row):
        return jnp.sum(jnp.where(same, row.astype(F32), 0.0), axis=1, keepdims=True).astype(I32)

    limit = [limits_ref[j : j + 1, :] for j in range(4)]
    limit_column = [as_column(row) for row in limit]
    spot = iota((reg_dev, patches), 1)
    spot_row, spot_col = spot >> 4, spot & 15
    inside = (
        (spot_row >= limit_column[0])
        & (spot_row < limit_column[1])
        & (spot_col >= limit_column[2])
        & (spot_col < limit_column[3])
    )
    region = iota((reg_dev, patches), 0)
    images = chunk // patches

    def pool_chunk(i):
        feature_copies[i].wait()
        mask = jnp.concatenate(
            [
                (
                    inside
                    & (region >= (i * images + m) * reg_img)
                    & (region < (i * images + m + 1) * reg_img)
                ).astype(F32)
                for m in range(images)
            ],
            axis=1,
        ).astype(BF16)
        term = dot(mask, feature[pl.ds(i * chunk, chunk)])
        pool[...] = term if i == 0 else pool[...] + term

    for i in range(n_feature):
        pool_chunk(i)
        hear(i + 1)
    pl.semaphore_wait(ready.at[0], 2)
    z_out[...] = fold(dot(dispatch, pool[...].astype(BF16))).astype(BF16)

    def block(ref, index):
        return ref.at[pl.ds(index * 2 * SLOT, 2 * SLOT)]

    z_copies = {}
    for dz in ISSUE:
        for dc in range(2):
            if (dz, dc) == (0, 0):
                continue
            there = (NZ - dz) % NZ
            copy = remote(
                block(z_out, dz * 2 + dc),
                block(z_in, there * 2 + dc),
                zf_send.at[dz, dc],
                zf_recv.at[there, dc],
                dz=dz,
                dc=dc,
            )
            copy.start()
            z_copies[dz, dc] = copy

    def to_unit(source, block, first, count):
        for i in range(first, first + count, 64):
            rows = pl.ds(max(block - 1, 0) * ph_dev + i, 64)
            them = source[rows].astype(F32)
            scale = lax.rsqrt(jnp.sum(them * them, axis=1, keepdims=True) + EPS)
            phrases[pl.ds(block * ph_dev + i, 64)] = (them * scale).astype(BF16)

    phrase_copy.wait()
    to_unit(raw, 0, 0, ph_dev)

    live = 4 * NZ * 2 * SLOT
    member_all = (shard_ref[...] == shard).astype(BF16)
    rank_all = dot(member_all, earlier).astype(BF16)
    slot = iota((live, n_dev), 0)
    k, xr, dc_, r_ = slot >> 6, (slot >> 4) & 3, (slot >> 3) & 1, slot & 7
    rel = jnp.zeros_like(k)
    for rel_z, at in PLACE.items():
        rel = jnp.where(k == at, rel_z, rel)
    from_z = (z + rel) & (NZ - 1)
    from_x = (x + xr) & (NX - 1)
    from_c = (c + dc_) & 1
    device = ((from_z * 2 + (from_x & 1)) * 2 + from_c) * 8 + (from_x >> 1) * 4 + y
    pick = (iota((live, n_dev), 1) == shard_row(device)).astype(BF16)
    member_slot = dot(pick, member_all)
    rank_slot = dot(pick, rank_all)
    wanted = r_[:, :reg_dev].astype(F32)
    local = (iota((live, reg_dev), 1) + 1).astype(F32)
    held = jnp.sum(
        jnp.where(rank_slot == wanted, member_slot * local, 0.0), axis=1, keepdims=True
    ).astype(I32)
    ids[...] = jnp.where(held > 0, device[:, :128] * reg_dev + held - 1, -1)

    collect = (iota((reg_dev, slots), 1) == as_column(goes)).astype(BF16)
    spot = iota((patches, reg_dev), 0)
    spot_row, spot_col = spot >> 4, spot & 15
    inside = (
        (spot_row >= limit[0])
        & (spot_row < limit[1])
        & (spot_col >= limit[2])
        & (spot_col < limit[3])
    )
    region = iota((patches, reg_dev), 1)
    for m in range(reg_dev // reg_img):
        mask = (inside & (region >= m * reg_img) & (region < (m + 1) * reg_img)).astype(BF16)
        spread[pl.ds(m * patches, patches)] = dot(mask, collect).astype(BF16)
    spread_copy = pltpu.make_async_copy(spread, spread_hbm, in_sem.at[4])
    spread_copy.start()

    x_copies = {}
    for step, rel in enumerate(NEAR):
        at = PLACE[rel]
        if step == LATE_OWN:
            ring_copies[2].start()
            ring_copies[3].start()
        if step == LATE_PASS:
            ring_copies[0].wait_recv()
            ring_copies[4].start()
            ring_copies[1].wait_recv()
            ring_copies[5].start()
        sides = []
        for dc in range(2):
            if (rel, dc) == (0, 0):
                got = block(z_out, 0)
            else:
                got = block(z_in, rel * 2 + dc)
                z_copies[(NZ - rel) % NZ, dc].wait_recv()
            sides.append(got[...].astype(F32))
        near, far = [
            jnp.concatenate(
                [side[p * SLOT : (p + 1) * SLOT] for side in sides], axis=0
            ).astype(BF16)
            for p in range(2)
        ]
        block(x_in, at * 4)[...] = near
        block(x_out, rel * 2)[...] = near
        block(x_out, rel * 2 + 1)[...] = far
        for dx in (2, 1, 3):
            there = NX - dx
            copy = remote(
                block(x_out, rel * 2 + dx % 2),
                block(x_in, at * 4 + there),
                xf_send.at[rel, dx - 1],
                xf_recv.at[rel, there - 1],
                dx=dx,
            )
            copy.start()
            x_copies[rel, dx] = copy

    named_copy.wait()
    sharp_copy.wait()
    shift_copy.wait()
    sharp, shift = sharp_ref[0], shift_ref[0]

    def arrive(rel):
        for dx in (2, 1, 3):
            x_copies[rel, dx].wait_recv()
        rows = pl.ds(PLACE[rel] * 64, 64)
        folded = x_in[rows].astype(F32)
        arrived = jnp.concatenate([folded, folded_columns(folded)], axis=1)
        inv = lax.rsqrt(jnp.sum(arrived * arrived, axis=1, keepdims=True) + EPS)
        regions[rows] = arrived.astype(BF16)
        inverse[rows] = jnp.broadcast_to(inv, (64, LANES))
        unit[rows] = (arrived * inv).astype(BF16)

    def pairs(rows, first, count):
        them = phrases[pl.ds(first, count)]
        scores = lax.dot_general(
            unit[rows], them, (((1,), (1,)), ((), ())), preferred_element_type=F32
        )
        mine = ids[rows]
        weights = []
        for j in range(count // LANES):
            block, inner = divmod(first + j * LANES, ph_dev)
            row = (me_phr // 4) * 12 + lax.rem(y + (0, 3, 1, 2)[block], NY) * 3 + inner // LANES
            logits = sharp * scores[:, j * LANES : (j + 1) * LANES] + shift
            positive = (mine == named[pl.ds(row, 1), :]).astype(F32)
            weights.append((jax.nn.sigmoid(logits) - positive).astype(BF16))
        return dot(jnp.concatenate(weights, axis=1), them)

    everything, far_half, near_half = pl.ds(0, live), pl.ds(0, live // 2), pl.ds(live // 2, live // 2)
    for rel in NEAR[:4]:
        arrive(rel)
    ring_copies[6].start()
    ring_copies[7].start()
    ring_copies[2].wait_recv()
    to_unit(ring_in, 1, 0, ph_dev)
    total[near_half] = pairs(near_half, 0, 2 * ph_dev)
    for rel in NEAR[4:]:
        arrive(rel)
    total[far_half] = pairs(far_half, 0, 2 * ph_dev)
    ring_copies[3].wait_recv()
    to_unit(ring_in, 2, 0, ph_dev)
    ring_copies[4].wait_recv()
    to_unit(ring_in, 3, 0, LANES)
    total[...] += pairs(everything, 2 * ph_dev, ph_dev + LANES)
    ring_copies[5].wait_recv()
    to_unit(ring_in, 3, 2 * LANES, LANES)
    ring_copies[6].wait_recv()
    ring_copies[7].wait_recv()
    to_unit(ring_in, 3, LANES, LANES)
    r_copies = {}

    def give(at):
        for begin, end in PARTS:
            if at == begin:
                rows = pl.ds(begin * 64, (end - begin) * 64)
                total[rows] += pairs(rows, 3 * ph_dev + LANES, 2 * LANES)
        rows = pl.ds(at * 64, 64)
        pull = sharp * total[rows]
        arrived = regions[rows].astype(F32)
        inv = inverse[rows][:, 0:1]
        radial = jnp.sum(arrived * pull, axis=1, keepdims=True)
        p_out[rows] = fold(inv * pull - (inv * inv * inv * radial) * arrived).astype(BF16)
        for dx in (2, 1, 3):
            there = NX - dx
            copy = remote(
                block(p_out, at * 4 + dx),
                block(p_in, at * 4 + there),
                xr_send.at[at, dx - 1],
                xr_recv.at[at, there - 1],
                dx=dx,
            )
            copy.start()
            r_copies[at, dx] = copy

    home_copies = {}
    for at in range(LEAD):
        give(at)
    for at, rel in enumerate(ORDER):
        for dx in (2, 1, 3):
            r_copies[at, dx].wait_recv()
        near = block(p_out, at * 4)[...].astype(F32) + block(p_in, at * 4 + 2)[...].astype(F32)
        far = block(p_in, at * 4 + 1)[...].astype(F32) + block(p_in, at * 4 + 3)[...].astype(F32)
        there = (NZ - rel) % NZ
        for dc in range(2):
            rows = slice(dc * SLOT, (dc + 1) * SLOT)
            block(s_out, at * 2 + dc)[...] = jnp.concatenate(
                [near[rows], far[rows]], axis=0
            ).astype(BF16)
            if (rel, dc) == (0, 0):
                stay = pltpu.make_async_copy(block(s_out, at * 2), block(back_hbm, 0), in_sem.at[5])
                stay.start()
                continue
            copy = remote(
                block(s_out, at * 2 + dc),
                block(back_hbm, there * 2 + dc),
                zr_send.at[rel, dc],
                zr_recv.at[there, dc],
                dz=rel,
                dc=dc,
            )
            copy.start()
            home_copies[rel, dc] = copy
        if at + LEAD < NZ:
            give(at + LEAD)

    for copy in home_copies.values():
        copy.wait_recv()
    stay.wait()
    spread_copy.wait()
    for copies in (ring_copies, z_copies.values(), x_copies.values(), r_copies.values(), home_copies.values()):
        for copy in copies:
            copy.wait_send()


def spread_kernel(spread_hbm, back_hbm, out_hbm, spread, back, last, staged, in_sems, out_sems):
    keep = back.shape[1]
    half = spread.shape[0] // 2
    back_copy = pltpu.make_async_copy(back_hbm, back, in_sems.at[2])
    back_copy.start()
    loads, stores = [], []
    for i in range(2):
        part = pl.ds(i * half, half)
        loads.append(pltpu.make_async_copy(spread_hbm.at[part], spread.at[part], in_sems.at[i]))
        loads[i].start()
    back_copy.wait()
    for first in range(0, keep + LANES, 2 * LANES):
        columns = pl.ds(first, min(2 * LANES, keep + LANES - first))
        if first == keep:
            last[...] = folded_columns(back[...].astype(F32)).astype(BF16)
        slots = back[:, columns] if first < keep else last[...]
        for i in range(2):
            if first == 0:
                loads[i].wait()
            part = pl.ds(i * half, half)
            staged[part, columns] = dot(spread[part], slots).astype(BF16)
            copy = pltpu.make_async_copy(
                staged.at[part, columns], out_hbm.at[part, columns], out_sems.at[len(stores)]
            )
            copy.start()
            stores.append(copy)
    for copy in stores:
        copy.wait()


def shards(features, limits, shard_index, named, phrases, sharpness, shift):
    images, patches, width = features.shape
    reg_dev, ph_dev = limits.shape[0], phrases.shape[0]
    n_dev = shard_index.shape[0] // reg_dev
    slots = NZ * 4 * SLOT
    live = slots * 2
    keep = width - LANES
    hbm = pl.BlockSpec(memory_space=pltpu.HBM)
    dma = pltpu.SemaphoreType.DMA
    back, spread = pl.pallas_call(
        exchange_kernel,
        out_shape=(
            jax.ShapeDtypeStruct((slots, keep), BF16),
            jax.ShapeDtypeStruct((images * patches, slots), BF16),
        ),
        in_specs=[hbm] * 7,
        out_specs=(hbm, hbm),
        scratch_shapes=[
            pltpu.VMEM((images * patches, width), BF16),
            pltpu.VMEM((ph_dev, width), BF16),
            pltpu.VMEM((24, LANES), I32),
            pltpu.SMEM((1,), F32),
            pltpu.SMEM((1,), F32),
            pltpu.VMEM((4, reg_dev), I32),
            pltpu.VMEM((n_dev * reg_dev // LANES, LANES), I32),
            pltpu.VMEM((n_dev, reg_dev), I32),
            pltpu.VMEM(((NY - 1) * ph_dev, width), BF16),
            pltpu.VMEM((NY * ph_dev, width), BF16),
            pltpu.VMEM((reg_dev, width), F32),
            pltpu.VMEM((slots, keep), BF16),
            pltpu.VMEM((slots, keep), BF16),
            pltpu.VMEM((slots, keep), BF16),
            pltpu.VMEM((live, keep), BF16),
            pltpu.VMEM((live, width), BF16),
            pltpu.VMEM((live, width), BF16),
            pltpu.VMEM((live, LANES), I32),
            pltpu.VMEM((live, LANES), F32),
            pltpu.VMEM((live, width), F32),
            pltpu.VMEM((live, keep), BF16),
            pltpu.VMEM((live, keep), BF16),
            pltpu.VMEM((slots, keep), BF16),
            pltpu.VMEM((images * patches, slots), BF16),
            dma((8,)),
            dma((4,)),
            dma((8,)),
            dma((8,)),
            dma((NZ, 2)),
            dma((NZ, 2)),
            dma((NZ, 3)),
            dma((NZ, 3)),
            dma((NZ, 3)),
            dma((NZ, 3)),
            dma((NZ, 2)),
            dma((NZ, 2)),
            pltpu.SemaphoreType.REGULAR((5,)),
        ],
        compiler_params=pltpu.CompilerParams(
            collective_id=0, has_side_effects=True, vmem_limit_bytes=62 * 2**20
        ),
    )(
        sharpness,
        shift,
        limits.T,
        shard_index.reshape(-1, 128),
        named.reshape(-1, 128),
        phrases,
        features.reshape(images * patches, width),
    )
    out = pl.pallas_call(
        spread_kernel,
        out_shape=jax.ShapeDtypeStruct((images * patches, width), BF16),
        in_specs=[hbm, hbm],
        out_specs=hbm,
        scratch_shapes=[
            pltpu.VMEM((images * patches, slots), BF16),
            pltpu.VMEM((slots, keep), BF16),
            pltpu.VMEM((slots, LANES), BF16),
            pltpu.VMEM((images * patches, width), BF16),
            dma((3,)),
            dma((2 * (width // LANES // 2 + 1),)),
        ],
        compiler_params=pltpu.CompilerParams(vmem_limit_bytes=62 * 2**20),
    )(spread, back)
    return out.reshape(images, patches, width)


def solution(mesh):
    return jax.shard_map(
        shards,
        mesh=mesh,
        in_specs=(
            P(("img", "phr"), None, None),
            P(("img", "phr"), None),
            P(),
            P(),
            P(("img", "phr"), None),
            P(),
            P(),
        ),
        out_specs=P(("img", "phr"), None, None),
        check_vma=False,
    )
```
